256 devices in a mesh: vel: 16 (over z, x_hi), cell: 16 (over x_lo, y, core).
Axes of the slice: x: 4 (x_hi: 2, x_lo: 2; x = x_hi * 2 + x_lo), y: 4, z: 8, core: 2. Of those that a mesh axis runs over, the one named last changes fastest.
Arguments:
- distribution: float32 [13824, 2048], P('vel', 'cell'), may hold values from 0.2 to 2
- pair_first: int32 [16, 16, 256], P('vel'), may hold values from 0 to 863
- pair_second: int32 [16, 16, 256], P('vel'), may hold values from 0 to 863
- pair_weight: float32 [16, 16, 256], P('vel'), may hold values from 0.05 to 0.5
- proj_pair: int32 [16, 16, 16, 64], P('vel'), may hold values from 0 to 255
- proj_target: int32 [16, 16, 16, 64], P(None, None, 'vel'), may hold values from 0 to 863
- proj_coef: float32 [16, 16, 16, 64], P(None, None, 'vel'), may hold values from 0.1 to 1
- slot_counts: int32 [16, 16, 16], P(None, None, 'vel'), may hold values from 16 to 64, as said below
Outputs:
- transported: float32 [13824, 2048], P('vel', 'cell')
- collision: float32 [13824, 2048], P('vel', 'cell')
The draws below stay inside these ranges and needn't reach their ends.
Inputs may be any that keep to these rules, and one draw needn't show every extreme that they name: slot_counts[s, p, o] live slots, counted from the first, in the list that source group s fills for partner group p and owner group o; for every offset (s - p) mod 16 one owner group gets exactly 64 live slots from every source group.
All inputs are finite; a program needn't handle non-finite values.
Results may differ from the reference program's by a relative error of at most 0.000054.
Values sent between devices are 32-bit elements; how exact they have to be, the bound alone decides.
A program may use at most 64 MiB of HBM per device.

```python
import math
import jax
import jax.numpy as jnp
from jax import lax

VSIDE = 24
PB = 256
V = 13824
GROUPS = 16
VB = 864
SLOTS = 64
CELLS = 2048


def draw_slot_counts(key, part):
    heavy_owner = jax.random.randint(jax.random.fold_in(key, 11), (GROUPS,), 0, GROUPS)
    base_count = jax.random.randint(jax.random.fold_in(key, 12), (GROUPS, GROUPS, GROUPS), SLOTS // 4, 3 * SLOTS // 4 + 1)
    source = jnp.arange(GROUPS)[:, None, None]
    partner = jnp.arange(GROUPS)[None, :, None]
    owner_index = jnp.arange(GROUPS)[None, None, :]
    offset = (source - partner) % GROUPS
    return jnp.where(owner_index == heavy_owner[offset], SLOTS, base_count).astype(jnp.int32)


def plant(result, own_key, low, top_value):
    spot = [jax.random.randint(jax.random.fold_in(own_key, axis), (), 0, length) for axis, length in enumerate(result.shape)]
    widest = result.shape.index(max(result.shape))
    next_to = spot[:widest] + [(spot[widest] + 1) % result.shape[widest]] + spot[widest + 1:]
    return result.at[tuple(spot)].set(low).at[tuple(next_to)].set(top_value)


def block_scale(own_key, shape, cuts, low, top_value):
    gain = 1.0
    for axis_at, blocks in cuts:
        steps = jax.random.uniform(jax.random.fold_in(jax.random.fold_in(own_key, 6), axis_at), (blocks,), jnp.float32, low / len(cuts), top_value / len(cuts))
        gain = gain * jnp.repeat(jnp.exp(steps), shape[axis_at] // blocks).reshape((-1,) + (1,) * (len(shape) - 1 - axis_at))
    return gain


def setup_inputs(seed: int = 0) -> dict:
    keys = jax.random.split(jax.random.key(seed), 9)
    distribution = jnp.clip(jnp.exp(math.log(2.0) - 2.3025851 * jax.random.uniform(keys[0], (V, CELLS), jnp.float32) ** block_scale(keys[0], (V, CELLS), ((0, 16), (1, 16)), -0.2, 0.2)), 0.2, 2.0)
    pair_first = plant(jax.random.randint(keys[1], (GROUPS, GROUPS, PB), 0, VB), jax.random.fold_in(keys[1], 1), 0, VB - 1).astype(jnp.int32)
    pair_second = plant(jax.random.randint(keys[2], (GROUPS, GROUPS, PB), 0, VB), jax.random.fold_in(keys[2], 1), 0, VB - 1).astype(jnp.int32)
    pair_weight = jnp.clip(jnp.exp(math.log(0.5) - 2.3025851 * jax.random.uniform(keys[3], (GROUPS, GROUPS, PB), jnp.float32) ** block_scale(keys[3], (GROUPS, GROUPS, PB), ((0, 16),), -0.2, 0.2)), 0.05, 0.5)
    proj_pair = plant(jax.random.randint(keys[4], (GROUPS, GROUPS, GROUPS, SLOTS), 0, PB), jax.random.fold_in(keys[4], 1), 0, PB - 1).astype(jnp.int32)
    proj_target = plant(jax.random.randint(keys[5], (GROUPS, GROUPS, GROUPS, SLOTS), 0, VB), jax.random.fold_in(keys[5], 1), 0, VB - 1).astype(jnp.int32)
    proj_coef = jnp.clip(0.1 + 0.9 * jax.random.uniform(keys[6], (GROUPS, GROUPS, GROUPS, SLOTS), jnp.float32) ** block_scale(keys[6], (GROUPS, GROUPS, GROUPS, SLOTS), ((2, 16),), -0.2, 0.2), 0.1, 1.0)
    slot_counts = draw_slot_counts(jax.random.fold_in(keys[8], 71), 0)
    return dict(distribution=distribution, pair_first=pair_first, pair_second=pair_second, pair_weight=pair_weight, proj_pair=proj_pair, proj_target=proj_target, proj_coef=proj_coef, slot_counts=slot_counts)


def reference(distribution, pair_first, pair_second, pair_weight, proj_pair, proj_target, proj_coef, slot_counts):
    block_rows = V // GROUPS
    node_index = jnp.arange(V, dtype=jnp.int32)
    first_axis = node_index // (VSIDE * VSIDE)
    courant = ((2 * first_axis - VSIDE + 1) / (2.0 * VSIDE)).astype(jnp.float32)[:, None]
    left_cell = jnp.roll(distribution, 1, axis=1)
    right_cell = jnp.roll(distribution, -1, axis=1)
    transported = distribution - jnp.maximum(courant, 0.0) * (distribution - left_cell) - jnp.minimum(courant, 0.0) * (right_cell - distribution)
    slot_index = jnp.arange(SLOTS, dtype=jnp.int32)
    owner_start = (jnp.arange(GROUPS, dtype=jnp.int32) * block_rows)[:, None]

    def advance(pair_block, totals):
        loss_sum, gain_sum = totals
        source = (pair_block // GROUPS).astype(jnp.int32)
        partner = (pair_block % GROUPS).astype(jnp.int32)
        first_node = pair_first[source, partner] + source * block_rows
        second_node = pair_second[source, partner] + partner * block_rows
        product = pair_weight[source, partner][:, None] * transported[first_node] * transported[second_node]
        loss_sum = loss_sum.at[first_node].add(product)
        live_slot = slot_index[None, :] < slot_counts[source, partner][:, None]
        factors = jnp.where(live_slot, proj_coef[source, partner], jnp.zeros_like(proj_coef[source, partner]))
        values = product[proj_pair[source, partner]] * factors[:, :, None]
        target = proj_target[source, partner] + owner_start
        gain_sum = gain_sum.at[target.reshape(-1)].add(values.reshape(-1, values.shape[-1]))
        return loss_sum, gain_sum

    zeros = jnp.zeros_like(transported)
    loss_sum, gain_sum = lax.fori_loop(0, GROUPS * GROUPS, advance, (zeros, zeros))
    return transported, gain_sum - loss_sum
```

```python
import functools

import jax
import jax.numpy as jnp
from jax import lax
from jax.experimental import pallas as pl
from jax.experimental.pallas import tpu as pltpu
from jax.sharding import PartitionSpec as P

VSIDE = 24
MESH = pl.DeviceIdType.MESH
ROWS = 864
HALF = 432
KPAD = 512
F32 = jnp.float32
BF16 = jnp.bfloat16


def split(value):
    high = value.astype(BF16)
    return high, (value - high.astype(F32)).astype(BF16)


def kernel(
    dist, first, second, weight, picks, target, coef,
    out_t, out_c,
    edge_out, edge_in, packed, ring, sends_idx, idx, pairs_i, pairs_w, target_all, coef_all,
    wts, xs, ys, prod, prod_row, lossq, lossq_row, gain, loss, final,
    edge_s, edge_r, part_s, part_r, ring_s, ring_r, zidx_s, zidx_r, xidx_s, xidx_r, cidx_s, cidx_r,
    arg_s, arg_r, fin_s, fin_r,
):
    vel = lax.axis_index("vel")
    cell = lax.axis_index("cell")
    z = vel // 2
    x = vel % 2
    y = 1 - x
    core = cell % 2
    sibling = cell + 1 - 2 * core
    left = (cell + 15) % 16
    right = (cell + 1) % 16

    def at_z(steps, col=None):
        return {"vel": ((z + steps + 8) % 8) * 2 + (x if col is None else col)}

    partner = at_z(0, y)
    barrier = pltpu.get_barrier_semaphore()
    for steps in range(1, 8):
        pl.semaphore_signal(barrier, inc=1, device_id=at_z(steps), device_id_type=MESH)
    pl.semaphore_signal(barrier, inc=1, device_id=partner, device_id_type=MESH)
    for side in (left, right):
        pl.semaphore_signal(barrier, inc=1, device_id={"cell": side}, device_id_type=MESH)

    def send(src, dst, s_sem, r_sem, device):
        copy = pltpu.make_async_remote_copy(
            src_ref=src, dst_ref=dst, send_sem=s_sem, recv_sem=r_sem, device_id=device, device_id_type=MESH
        )
        copy.start()
        return copy

    lane8 = lax.broadcasted_iota(jnp.int32, (8, 128), 1)
    sub8 = lax.broadcasted_iota(jnp.int32, (8, 128), 0)
    pick = jnp.where(lane8 == 127 * sub8, 1.0, 0.0).astype(F32)
    edges = lax.dot_general(
        pick, dist[...], (((1,), (1,)), ((), ())), precision=lax.Precision.HIGHEST, preferred_element_type=F32
    )
    edge_out[0] = edges[1:2]
    edge_out[1] = edges[0:1]

    for b in range(8):
        take = picks[core, b]
        low = take & 127
        upper = take >= 128
        lane_first = lane8 < 64
        for kind, table in enumerate((first, second, weight)):
            rows = []
            for half in range(2):
                group = 2 * b + (half + x) % 2
                for part in range(2):
                    row = table[pl.ds(group * 2 + part, 1), :]
                    row = jnp.broadcast_to(row, (8, 128))
                    rows.append(jnp.take_along_axis(row, low, axis=1, mode="promise_in_bounds"))
            value = jnp.where(
                lane_first, jnp.where(upper, rows[1], rows[0]), jnp.where(upper, rows[3], rows[2])
            ).astype(F32)
            for owner in range(8):
                sends_idx[owner, pl.ds(kind * 8 + b, 1), :] = value[owner : owner + 1]

    pl.semaphore_wait(barrier, 10)

    edge_copies = [
        send(edge_out.at[0], edge_in.at[0], edge_s.at[0], edge_r.at[0], {"cell": right}),
        send(edge_out.at[1], edge_in.at[1], edge_s.at[1], edge_r.at[1], {"cell": left}),
    ]
    z_copies = [
        send(sends_idx.at[(z + k) % 8], idx.at[core, x, z], zidx_s.at[k], zidx_r.at[k], at_z(k)) for k in range(1, 8)
    ]
    idx[core, x, pl.ds(z, 1)] = sends_idx[pl.ds(z, 1)]
    pairs_i[x, 0] = first[...]
    pairs_i[x, 1] = second[...]
    pairs_w[x] = weight[...]
    arg_copies = [
        send(first, pairs_i.at[x, 0], arg_s.at[0], arg_r.at[0], partner),
        send(second, pairs_i.at[x, 1], arg_s.at[1], arg_r.at[1], partner),
        send(weight, pairs_w.at[x], arg_s.at[2], arg_r.at[2], partner),
        send(coef, coef_all.at[x], arg_s.at[3], arg_r.at[3], partner),
        send(target, target_all.at[x], arg_s.at[4], arg_r.at[4], partner),
    ]
    coef_all[x] = coef[...]
    target_all[x] = target[...]

    for copy in edge_copies:
        copy.wait_recv()
    node = vel * ROWS + lax.broadcasted_iota(jnp.int32, (ROWS, 128), 0)
    courant = (2 * (node // (VSIDE * VSIDE)) - VSIDE + 1).astype(F32) / (2.0 * VSIDE)
    lane = lax.broadcasted_iota(jnp.int32, (ROWS, 128), 1)
    here = dist[...]

    def column(row):
        return jnp.broadcast_to(row, (8, ROWS)).T[:, 0:1]

    before = jnp.where(lane == 0, column(edge_in[0]), pltpu.roll(here, 1, axis=1))
    after = jnp.where(lane == 127, column(edge_in[1]), pltpu.roll(here, 127, axis=1))
    moved = here - jnp.maximum(courant, 0.0) * (here - before) - jnp.minimum(courant, 0.0) * (after - here)
    out_t[...] = moved
    top, low = moved[:HALF], moved[HALF:]
    lane_low = lax.broadcasted_iota(jnp.int32, (HALF, 128), 1) < 64
    packed[0] = jnp.where(lane_low, top, pltpu.roll(low, 64, axis=1))
    packed[1] = jnp.where(lane_low, pltpu.roll(top, 64, axis=1), low)
    part_copy = send(packed.at[y], ring.at[0, x], part_s, part_r, partner)
    ring[0, pl.ds(x, 1)] = packed[pl.ds(x, 1)]

    def ring_copy(way, step, src_m, dst_m, group):
        return pltpu.make_async_remote_copy(
            src_ref=ring.at[src_m, group],
            dst_ref=ring.at[dst_m, group],
            send_sem=ring_s.at[way, step],
            recv_sem=ring_r.at[way, step],
            device_id=at_z(1 - 2 * way),
            device_id_type=MESH,
        )

    ring_copy(0, 1, 0, 1, x).start()
    ring_copy(1, 1, 0, 2, x).start()

    gain[...] = jnp.zeros_like(gain)
    loss[...] = jnp.zeros_like(loss)
    wts[...] = jnp.zeros_like(wts)

    part_copy.wait_send()
    part_copy.wait_recv()
    ring_copy(0, 2, 0, 1, y).start()
    ring_copy(1, 2, 0, 2, y).start()

    for copy in z_copies:
        copy.wait_recv()
    x_copy = send(idx.at[core, x], idx.at[core, x], xidx_s, xidx_r, partner)
    for copy in arg_copies:
        copy.wait_recv()
    x_copy.wait_recv()
    c_copy = send(idx.at[core], idx.at[core], cidx_s, cidx_r, {"cell": sibling})
    c_copy.wait_recv()

    def place(m):
        return (z + (m % 2) * (8 - (m + 1) // 2) + (1 - m % 2) * (m // 2)) % 8

    slot_iota = lax.broadcasted_iota(jnp.int32, (KPAD, 18 * 128), 0).astype(F32)
    row_low = lax.broadcasted_iota(jnp.int32, (1, 128), 1) < 64

    def gather_group(m, group, sequence):
        zz = place(m)
        actual = 2 * zz + group
        turned = ring[m, group].T
        high, rest = split(turned)
        wts[0:128, 0:HALF] = high
        wts[128:256, 0:HALF] = rest

        def gather(e, carry):
            rows = [idx[e, group, zz, b : b + 1, :] for b in range(8)]
            for a in range(8):
                even = idx[e, 0, a, pl.ds(8 + zz, 1), :]
                odd = idx[e, 1, a, pl.ds(8 + zz, 1), :]
                rows.append(jnp.where(row_low == (group == 0), even, odd))
            rows.append(pairs_i[e, 1, pl.ds(actual * 2, 1), :].astype(F32))
            rows.append(pairs_i[e, 1, pl.ds(actual * 2 + 1, 1), :].astype(F32))
            nodes = jnp.concatenate(rows, axis=1)
            upper = nodes >= float(HALF)
            local = jnp.where(upper, nodes - float(HALF), nodes)
            one_hot = jnp.where(slot_iota == local, 1.0, 0.0).astype(BF16)
            found = jnp.dot(wts[...], one_hot, preferred_element_type=F32)
            found = found[0:128] + found[128:256]
            found = jnp.where(upper, found[64:128], found[0:64])
            for b in range(8):
                scale = idx[e, group, zz, 16 + b : 17 + b, :] * coef_all[e, actual, b : b + 1, :]
                xs[m, group, e, b] = found[:, b * 128 : b * 128 + 128] * scale
                ys[m, group, e, b] = found[:, 1024 + b * 128 : 1024 + b * 128 + 128]
            for part in range(2):
                term = found[:, 2048 + part * 128 : 2048 + part * 128 + 128]
                term = term * pairs_w[e, pl.ds(actual * 2 + part, 1), :]
                goal = pairs_i[e, 0, pl.ds(actual * 2 + part, 1), :]
                put(lossq, lossq_row, e, (sequence % 4) * 2 + part, term, goal)
            return carry

        lax.fori_loop(0, 2, gather, 0)

    def put(queue, queue_row, e, tile, term, goal):
        upper = goal >= HALF
        high, rest = split(jnp.concatenate([jnp.where(upper, 0.0, term), jnp.where(upper, term, 0.0)], axis=0))
        queue[e, tile, 0:128] = high
        queue[e, tile, 128:256] = rest
        queue_row[e, tile] = jnp.where(upper, goal - HALF, goal)

    def add_up(total, queue, queue_row, e, tiles):
        goal = jnp.concatenate([queue_row[e, i] for i in range(tiles)], axis=1)
        node_iota = lax.broadcasted_iota(jnp.int32, (HALF, tiles * 128), 0)
        one_hot = jnp.where(node_iota == goal, 1.0, 0.0).astype(BF16)
        terms = jnp.concatenate([queue[e, i] for i in range(tiles)], axis=1)
        total[e] += lax.dot_general(one_hot, terms, (((1,), (1,)), ((), ())), preferred_element_type=F32)

    tile_low = lax.broadcasted_iota(jnp.int32, (64, 128), 1) < 64

    def chunk(c, carry):
        def one_owner(e, inner):
            def block(i, deep):
                n = c * 8 + i
                m = sum([(n + 64 - k * k) // 64 for k in range(1, 8)])
                d = n - m * m
                later = (d + 7 - m) // 8
                ma = (1 - later) * m + later * (d - m - 1)
                mb = (1 - later) * d + later * m
                za, zb = place(ma), place(mb)
                even, odd = xs[ma, 0, e, zb], xs[ma, 1, e, zb]
                put(prod, prod_row, e, 2 * i, jnp.where(tile_low, even, odd) * ys[mb, 0, e, za],
                    target_all[e, za, zb, 0:1, :])
                put(prod, prod_row, e, 2 * i + 1, jnp.where(tile_low, odd, even) * ys[mb, 1, e, za],
                    target_all[e, za, zb, 1:2, :])
                return deep

            lax.fori_loop(0, 8, block, 0)
            add_up(gain, prod, prod_row, e, 16)
            return inner

        lax.fori_loop(0, 2, one_owner, 0)
        return carry

    def step(t, carry):
        k = (t + 1) // 2
        group = (x + t + 1) % 2

        @pl.when(t >= 1)
        def _():
            last = t // 7
            m0 = 2 * k - 1
            m1 = 2 * k - last
            ring_copy(0, t, m0, m0, (1 - last) * group).wait_recv()
            ring_copy(1, t, m1, m1, (1 - last) * group + last).wait_recv()

        @pl.when((t >= 1) & (t <= 4))
        def _():
            ring_copy(0, t + 2, 2 * k - 1, 2 * k + 1, group).start()
            ring_copy(1, t + 2, 2 * k, 2 * k + 2, group).start()

        @pl.when((t >= 5) & (t <= 6))
        def _():
            ring_copy(group, 7, 5 + group, 7, group).start()

        def one(i, inner):
            ends = (t // 7) + (7 - t) // 7
            m = (1 - ends) * (2 * k - 1 + i) + (t // 7) * 7
            g = (1 - ends) * group + ends * i
            gather_group(m, g, 2 * t + i)
            return inner

        lax.fori_loop(0, 2, one, 0)

        @pl.when(t % 2 == 1)
        def _():
            def lossy(e, inner):
                add_up(loss, lossq, lossq_row, e, 8)
                return inner

            lax.fori_loop(0, 2, lossy, 0)

        def ready(t):
            return (t // 2) * (t // 2 + 1) // 2 + 2 * (t // 7)

        before_t = jnp.where(t > 0, ready(jnp.maximum(t - 1, 0)), 0)
        lax.fori_loop(before_t, ready(t), chunk, 0)
        return carry

    lax.fori_loop(0, 8, step, 0)

    def finish(e):
        g = gain[e]
        s = loss[e]
        return g[:, 0:128] + g[:, 128:256] - ring[0, e] * (s[:, 0:128] + s[:, 128:256])

    packed[0] = finish(y)
    fin_copy = send(packed.at[0], final.at[x], fin_s, fin_r, partner)
    final[pl.ds(x, 1)] = finish(x)[None]
    fin_copy.wait_recv()
    lo, hi = final[0], final[1]
    out_c[0:HALF, :] = jnp.where(lane_low, lo, pltpu.roll(hi, 64, axis=1))
    out_c[HALF:ROWS, :] = jnp.where(lane_low, pltpu.roll(lo, 64, axis=1), hi)

    for copy in edge_copies + z_copies + arg_copies + [x_copy, c_copy, fin_copy]:
        copy.wait_send()

    def drain(t, carry):
        m0 = 0
        ring_copy(0, t, m0, m0, 0).wait_send()
        ring_copy(1, t, m0, m0, 0).wait_send()
        return carry

    lax.fori_loop(1, 8, drain, 0)


def on_device(distribution, pair_first, pair_second, pair_weight, proj_pair, proj_target, proj_coef, slot_counts):
    x = lax.axis_index("vel") % 2
    picks = proj_pair.reshape(8, 2, 8, 2, 64)
    picks = jnp.where(x == 1, picks[:, ::-1], picks)
    picks = picks.transpose(3, 0, 2, 1, 4).reshape(2, 8, 8, 128)
    live = jnp.arange(64, dtype=jnp.int32) < slot_counts[:, :, :, None]
    coef = jnp.where(live, proj_coef, 0.0).reshape(8, 2, 8, 2, 64)
    coef = jnp.stack([coef[:, 0], coef[:, 1, :, ::-1]], axis=1).reshape(16, 8, 128)
    goal = proj_target.reshape(8, 2, 8, 2, 64)
    goal = jnp.stack([goal[:, :, :, 0], goal[:, ::-1, :, 1]], axis=1)
    goal = goal.transpose(0, 3, 1, 2, 4).reshape(8, 8, 2, 128)

    vmem = pl.BlockSpec(memory_space=pltpu.VMEM)
    dma = pltpu.SemaphoreType.DMA
    return pl.pallas_call(
        kernel,
        out_shape=(jax.ShapeDtypeStruct((ROWS, 128), F32), jax.ShapeDtypeStruct((ROWS, 128), F32)),
        in_specs=[vmem] * 7,
        out_specs=(vmem, vmem),
        scratch_shapes=[
            pltpu.VMEM((2, 1, ROWS), F32),
            pltpu.VMEM((2, 1, ROWS), F32),
            pltpu.VMEM((2, HALF, 128), F32),
            pltpu.VMEM((8, 2, HALF, 128), F32),
            pltpu.VMEM((8, 24, 128), F32),
            pltpu.VMEM((2, 2, 8, 24, 128), F32),
            pltpu.VMEM((2, 2, 32, 128), jnp.int32),
            pltpu.VMEM((2, 32, 128), F32),
            pltpu.VMEM((2, 8, 8, 2, 128), jnp.int32),
            pltpu.VMEM((2, 16, 8, 128), F32),
            pltpu.VMEM((256, KPAD), BF16),
            pltpu.VMEM((8, 2, 2, 8, 64, 128), F32),
            pltpu.VMEM((8, 2, 2, 8, 64, 128), F32),
            pltpu.VMEM((2, 16, 256, 128), BF16),
            pltpu.VMEM((2, 16, 1, 128), jnp.int32),
            pltpu.VMEM((2, 8, 256, 128), BF16),
            pltpu.VMEM((2, 8, 1, 128), jnp.int32),
            pltpu.VMEM((2, HALF, 256), F32),
            pltpu.VMEM((2, HALF, 256), F32),
            pltpu.VMEM((2, HALF, 128), F32),
            dma((2,)), dma((2,)), dma, dma, dma((2, 8)), dma((2, 8)), dma((8,)), dma((8,)), dma, dma, dma, dma,
            dma((5,)), dma((5,)), dma, dma,
        ],
        compiler_params=pltpu.CompilerParams(
            collective_id=0, has_side_effects=True, vmem_limit_bytes=60 << 20
        ),
    )(
        distribution,
        pair_first.reshape(32, 128),
        pair_second.reshape(32, 128),
        pair_weight.reshape(32, 128),
        picks,
        goal,
        coef,
    )


def solution(mesh):
    in_specs = (
        P("vel", "cell"),
        P("vel", None, None),
        P("vel", None, None),
        P("vel", None, None),
        P("vel", None, None, None),
        P(None, None, "vel", None),
        P(None, None, "vel", None),
        P(None, None, "vel"),
    )
    out_specs = (P("vel", "cell"), P("vel", "cell"))
    return jax.shard_map(
        on_device, mesh=mesh, in_specs=in_specs, out_specs=out_specs, check_vma=False
    )
```

```python
import functools

import jax
import jax.numpy as jnp
from jax import lax
from jax.experimental import pallas as pl
from jax.experimental.pallas import tpu as pltpu
from jax.sharding import PartitionSpec as P

VSIDE = 24
MESH = pl.DeviceIdType.MESH
ROWS = 864
HALF = 432
KPAD = 512
F32 = jnp.float32
BF16 = jnp.bfloat16


def split(value):
    high = value.astype(BF16)
    return high, (value - high.astype(F32)).astype(BF16)


def kernel(
    dist, first, second, weight, picks, target, coef, counts,
    out_t, out_c,
    edge_out, edge_in, packed, ring, sends_idx, idx, pairs, args, wts, xs, ys, lossq, lossq_row, gain, loss, final,
    edge_s, edge_r, part_s, part_r, ring_s, ring_r, zidx_s, zidx_r, xs_s, xs_r, cs_s, cs_r, fin_s, fin_r,
):
    vel = lax.axis_index("vel")
    cell = lax.axis_index("cell")
    z = vel // 2
    x = vel % 2
    y = 1 - x
    core = cell % 2
    left = (cell + 15) % 16
    right = (cell + 1) % 16

    def at_z(steps, col=None):
        return {"vel": ((z + steps + 8) % 8) * 2 + (x if col is None else col)}

    partner = at_z(0, y)
    sibling = {"cell": cell + 1 - 2 * core}
    barrier = pltpu.get_barrier_semaphore()
    for steps in range(1, 8):
        pl.semaphore_signal(barrier, inc=1, device_id=at_z(steps), device_id_type=MESH)
    pl.semaphore_signal(barrier, inc=1, device_id=partner, device_id_type=MESH)
    for side in (left, right):
        pl.semaphore_signal(barrier, inc=1, device_id={"cell": side}, device_id_type=MESH)

    def send(src, dst, s_sem, r_sem, device):
        copy = pltpu.make_async_remote_copy(
            src_ref=src, dst_ref=dst, send_sem=s_sem, recv_sem=r_sem, device_id=device, device_id_type=MESH
        )
        copy.start()
        return copy

    lane8 = lax.broadcasted_iota(jnp.int32, (8, 128), 1)
    sub8 = lax.broadcasted_iota(jnp.int32, (8, 128), 0)
    pick = jnp.where(lane8 == 127 * sub8, 1.0, 0.0).astype(F32)
    edges = lax.dot_general(
        pick, dist[...], (((1,), (1,)), ((), ())), precision=lax.Precision.HIGHEST, preferred_element_type=F32
    )
    edge_out[0] = edges[1:2]
    edge_out[1] = edges[0:1]

    for half in range(2):
        rows = slice(half * 8, half * 8 + 8)
        pairs[half, x, 0] = first[0, rows, :].astype(F32)
        pairs[half, x, 1] = second[0, rows, :].astype(F32)
        pairs[half, x, 2] = weight[0, rows, :]

    pl.semaphore_wait(barrier, 10)

    edge_copies = [
        send(edge_out.at[0], edge_in.at[0], edge_s.at[0], edge_r.at[0], {"cell": right}),
        send(edge_out.at[1], edge_in.at[1], edge_s.at[1], edge_r.at[1], {"cell": left}),
    ]
    pairs_copy = send(pairs.at[core, x], pairs.at[core, x], xs_s.at[0], xs_r.at[0], partner)

    for b in range(8):
        groups = [2 * b + (half + x) % 2 for half in range(2)]
        take = jnp.concatenate([picks[0, group, pl.ds(core, 8, stride=2), :] for group in groups], axis=1)
        low = take & 127
        upper = take >= 128
        lane_first = lane8 < 64
        for kind, table in enumerate((first, second, weight)):
            rows = []
            for group in groups:
                row = table[0, pl.ds(group, 1), :]
                for part in range(2):
                    piece = jnp.broadcast_to(row[:, part * 128 : part * 128 + 128], (8, 128))
                    rows.append(jnp.take_along_axis(piece, low, axis=1, mode="promise_in_bounds"))
            value = jnp.where(
                lane_first, jnp.where(upper, rows[1], rows[0]), jnp.where(upper, rows[3], rows[2])
            ).astype(F32)
            for owner in range(8):
                sends_idx[owner, pl.ds(kind * 8 + b, 1), :] = value[owner : owner + 1]
    z_copies = [
        send(sends_idx.at[(z + k) % 8], idx.at[core, x, z], zidx_s.at[k], zidx_r.at[k], at_z(k)) for k in range(1, 8)
    ]
    idx[core, x, pl.ds(z, 1)] = sends_idx[pl.ds(z, 1)]

    for copy in edge_copies:
        copy.wait_recv()
    node = vel * ROWS + lax.broadcasted_iota(jnp.int32, (ROWS, 128), 0)
    courant = (2 * (node // (VSIDE * VSIDE)) - VSIDE + 1).astype(F32) / (2.0 * VSIDE)
    lane = lax.broadcasted_iota(jnp.int32, (ROWS, 128), 1)
    here = dist[...]

    def column(row):
        return jnp.broadcast_to(row, (8, ROWS)).T[:, 0:1]

    before = jnp.where(lane == 0, column(edge_in[0]), pltpu.roll(here, 1, axis=1))
    after = jnp.where(lane == 127, column(edge_in[1]), pltpu.roll(here, 127, axis=1))
    moved = here - jnp.maximum(courant, 0.0) * (here - before) - jnp.minimum(courant, 0.0) * (after - here)
    out_t[...] = moved
    top, low = moved[:HALF], moved[HALF:]
    lane_low = lax.broadcasted_iota(jnp.int32, (HALF, 128), 1) < 64
    packed[0] = jnp.where(lane_low, top, pltpu.roll(low, 64, axis=1))
    packed[1] = jnp.where(lane_low, pltpu.roll(top, 64, axis=1), low)
    ring[0, pl.ds(x, 1)] = packed[pl.ds(x, 1)]

    def ring_copy(way, step, src_m, dst_m, group):
        return pltpu.make_async_remote_copy(
            src_ref=ring.at[src_m, group],
            dst_ref=ring.at[dst_m, group],
            send_sem=ring_s.at[way, step],
            recv_sem=ring_r.at[way, step],
            device_id=at_z(1 - 2 * way),
            device_id_type=MESH,
        )

    ring_copy(0, 1, 0, 1, x).start()
    ring_copy(1, 1, 0, 2, x).start()
    part_copy = send(packed.at[y], ring.at[0, x], part_s, part_r, partner)

    slot = lax.broadcasted_iota(jnp.int32, (8, 64), 1)
    for s in range(16):
        rows = []
        for half in range(2):
            every = pl.ds((half + s) % 2, 8, stride=2)
            rows.append(jnp.where(slot < counts[s, every, :], coef[s, every, 0, :], 0.0))
        args[0, x, s * 8 : s * 8 + 8] = jnp.concatenate(rows, axis=1)
    for a in range(8):
        for tile in range(2):
            every = pl.ds(tile, 8, stride=2)
            rows = [target[2 * a + (half + tile) % 2, every, 0, :] for half in range(2)]
            start = a * 16 + tile * 8
            args[1, x, start : start + 8] = jnp.concatenate(rows, axis=1).astype(F32)
    args_copy = send(args.at[core, x], args.at[core, x], xs_s.at[1], xs_r.at[1], partner)

    for copy in z_copies:
        copy.wait_recv()
    idx_copy = send(idx.at[core, x], idx.at[core, x], xs_s.at[2], xs_r.at[2], partner)

    gain[...] = jnp.zeros_like(gain)
    loss[...] = jnp.zeros_like(loss)
    wts[...] = jnp.zeros_like(wts)

    part_copy.wait_recv()
    ring_copy(0, 2, 0, 1, y).start()
    ring_copy(1, 2, 0, 2, y).start()

    pairs_copy.wait_recv()
    pairs_on = send(pairs.at[core, y], pairs.at[core, y], cs_s.at[0], cs_r.at[0], sibling)
    args_copy.wait_recv()
    args_on = send(args.at[core, y], args.at[core, y], cs_s.at[1], cs_r.at[1], sibling)
    idx_copy.wait_recv()
    idx_on = send(idx.at[core], idx.at[core], cs_s.at[2], cs_r.at[2], sibling)
    pairs_on.wait_recv()
    args_on.wait_recv()
    idx_on.wait_recv()

    def place(m):
        return (z + (m % 2) * (8 - (m + 1) // 2) + (1 - m % 2) * (m // 2)) % 8

    row_low = lax.broadcasted_iota(jnp.int32, (1, 128), 1) < 64

    def split_terms(term, upper):
        high, rest = split(jnp.concatenate([jnp.where(upper, 0.0, term), jnp.where(upper, term, 0.0)], axis=0))
        return jnp.concatenate([high, rest], axis=0)

    def gather_group(i, m, group, sequence, e):
        zz = place(m)
        actual = 2 * zz + group
        rows = [idx[e, group, zz, b : b + 1, :] for b in range(8)]
        for a in range(8):
            even = idx[e, 0, a, pl.ds(8 + zz, 1), :]
            odd = idx[e, 1, a, pl.ds(8 + zz, 1), :]
            rows.append(jnp.where(row_low == (group == 0), even, odd))
        pair_half, pair_row = zz // 4, pl.ds(actual % 8, 1)
        rows.append(pairs[pair_half, e, 1, pair_row, :])
        nodes = jnp.concatenate(rows, axis=1)
        upper = nodes >= float(HALF)
        local = jnp.where(upper, nodes - float(HALF), nodes)
        slot_iota = lax.broadcasted_iota(jnp.int32, (KPAD, 18 * 128), 0).astype(F32)
        one_hot = jnp.where(slot_iota == local, 1.0, 0.0).astype(BF16)
        found = jnp.dot(wts[i], one_hot, preferred_element_type=F32)
        found = found[0:128] + found[128:256]
        found = jnp.where(upper, found[64:128], found[0:64])
        for b in range(8):
            scale = idx[e, group, zz, 16 + b : 17 + b, :] * args[0, e, pl.ds(actual * 8 + b, 1), :]
            xs[m, group, e, b] = found[:, b * 128 : b * 128 + 128] * scale
            ys[m, group, e, b] = found[:, 1024 + b * 128 : 1024 + b * 128 + 128]
        share = pairs[pair_half, e, 2, pair_row, :]
        goal = pairs[pair_half, e, 0, pair_row, :]
        upper = goal >= float(HALF)
        terms = split_terms(found[:, 2048:2304] * share, upper)
        goal = jnp.where(upper, goal - float(HALF), goal)
        for part in range(2):
            tile = (sequence % 4) * 2 + part
            lossq[e, tile] = terms[:, part * 128 : part * 128 + 128]
            lossq_row[e, tile] = goal[:, part * 128 : part * 128 + 128]

    def scatter(goals, terms):
        goal = jnp.concatenate(goals, axis=1)
        node_iota = lax.broadcasted_iota(jnp.int32, (HALF, len(goals) * 128), 0).astype(F32)
        one_hot = jnp.where(node_iota == goal, 1.0, 0.0).astype(BF16)
        return lax.dot_general(
            one_hot, jnp.concatenate(terms, axis=1), (((1,), (1,)), ((), ())), preferred_element_type=F32
        )

    tile_low = lax.broadcasted_iota(jnp.int32, (64, 128), 1) < 64

    def chunk(c, e):
        goals, terms = [], []
        for i in range(8):
            n = c * 8 + i
            m = sum([(n + 64 - k * k) // 64 for k in range(1, 8)])
            d = n - m * m
            later = (d + 7 - m) // 8
            ma = (1 - later) * m + later * (d - m - 1)
            mb = (1 - later) * d + later * m
            za, zb = place(ma), place(mb)
            even, odd = xs[ma, 0, e, zb], xs[ma, 1, e, zb]
            for tile in range(2):
                mine = jnp.where(tile_low, even, odd) if tile == 0 else jnp.where(tile_low, odd, even)
                goal = args[1, e, pl.ds(za * 16 + tile * 8 + zb, 1), :]
                upper = goal >= float(HALF)
                terms.append(split_terms(mine * ys[mb, tile, e, za], upper))
                goals.append(jnp.where(upper, goal - float(HALF), goal))
        gain[e] += scatter(goals, terms)
        return e

    def finish(e):
        g = gain[e]
        s = loss[e]
        return g[:, 0:128] + g[:, 128:256] - ring[0, e] * (s[:, 0:128] + s[:, 128:256])

    def final_copy():
        return pltpu.make_async_remote_copy(
            src_ref=packed.at[0], dst_ref=final.at[x], send_sem=fin_s, recv_sem=fin_r, device_id=partner,
            device_id_type=MESH,
        )

    part_copy.wait_send()

    def step(t, carry):
        k = (t + 1) // 2
        group = (x + t + 1) % 2
        last = t // 7

        @pl.when(t >= 1)
        def _():
            m0 = 2 * k - 1
            m1 = 2 * k - last
            ring_copy(0, t, m0, m0, (1 - last) * group).wait_recv()
            ring_copy(1, t, m1, m1, (1 - last) * group + last).wait_recv()

        @pl.when((t >= 1) & (t <= 4))
        def _():
            ring_copy(0, t + 2, 2 * k - 1, 2 * k + 1, group).start()
            ring_copy(1, t + 2, 2 * k, 2 * k + 2, group).start()

        @pl.when((t >= 5) & (t <= 6))
        def _():
            ring_copy(group, 7, 5 + group, 7, group).start()

        ends = last + (7 - t) // 7
        arrived = []
        for i in range(2):
            m = (1 - ends) * (2 * k - 1 + i) + last * 7
            g = (1 - ends) * group + ends * i
            arrived.append((m, g))
            high, rest = split(ring[m, g].T)
            wts[i, 0:128, 0:HALF] = high
            wts[i, 128:256, 0:HALF] = rest

        def ready(t):
            return (t // 2) * (t // 2 + 1) // 2 + 2 * (t // 7)

        from_chunk = ready(t - 1 + (7 - t) // 7)

        def one_owner(turn, inner):
            e = (y + turn) % 2
            for i in range(2):
                gather_group(i, *arrived[i], 2 * t + i, e)

            @pl.when(t % 2 == 1)
            def _():
                loss[e] += scatter([lossq_row[e, i] for i in range(8)], [lossq[e, i] for i in range(8)])

            lax.fori_loop(from_chunk, ready(t), chunk, e)

            @pl.when((t == 7) & (turn == 0))
            def _():
                packed[0] = finish(y)
                final_copy().start()

            return inner

        lax.fori_loop(0, 2, one_owner, 0)
        return carry

    lax.fori_loop(0, 8, step, 0)

    final[pl.ds(x, 1)] = finish(x)[None]
    final_copy().wait_recv()
    lo, hi = final[0], final[1]
    out_c[0:HALF, :] = jnp.where(lane_low, lo, pltpu.roll(hi, 64, axis=1))
    out_c[HALF:ROWS, :] = jnp.where(lane_low, pltpu.roll(lo, 64, axis=1), hi)

    final_copy().wait_send()
    for copy in edge_copies + z_copies + [pairs_copy, args_copy, idx_copy, pairs_on, args_on, idx_on]:
        copy.wait_send()

    def drain(t, carry):
        ring_copy(0, t, 0, 0, 0).wait_send()
        ring_copy(1, t, 0, 0, 0).wait_send()
        return carry

    lax.fori_loop(1, 8, drain, 0)


def on_device(distribution, pair_first, pair_second, pair_weight, proj_pair, proj_target, proj_coef, slot_counts):
    vmem = pl.BlockSpec(memory_space=pltpu.VMEM)
    dma = pltpu.SemaphoreType.DMA
    return pl.pallas_call(
        kernel,
        out_shape=(jax.ShapeDtypeStruct((ROWS, 128), F32), jax.ShapeDtypeStruct((ROWS, 128), F32)),
        in_specs=[vmem] * 8,
        out_specs=(vmem, vmem),
        scratch_shapes=[
            pltpu.VMEM((2, 1, ROWS), F32),
            pltpu.VMEM((2, 1, ROWS), F32),
            pltpu.VMEM((2, HALF, 128), F32),
            pltpu.VMEM((8, 2, HALF, 128), F32),
            pltpu.VMEM((8, 24, 128), F32),
            pltpu.VMEM((2, 2, 8, 24, 128), F32),
            pltpu.VMEM((2, 2, 3, 8, 256), F32),
            pltpu.VMEM((2, 2, 128, 128), F32),
            pltpu.VMEM((2, 256, KPAD), BF16),
            pltpu.VMEM((8, 2, 2, 8, 64, 128), F32),
            pltpu.VMEM((8, 2, 2, 8, 64, 128), F32),
            pltpu.VMEM((2, 8, 256, 128), BF16),
            pltpu.VMEM((2, 8, 1, 128), F32),
            pltpu.VMEM((2, HALF, 256), F32),
            pltpu.VMEM((2, HALF, 256), F32),
            pltpu.VMEM((2, HALF, 128), F32),
            dma((2,)), dma((2,)), dma, dma, dma((2, 8)), dma((2, 8)), dma((8,)), dma((8,)), dma((3,)), dma((3,)),
            dma((3,)), dma((3,)), dma, dma,
        ],
        compiler_params=pltpu.CompilerParams(
            collective_id=0, has_side_effects=True, vmem_limit_bytes=60 << 20
        ),
    )(distribution, pair_first, pair_second, pair_weight, proj_pair, proj_target, proj_coef, slot_counts)


def solution(mesh):
    in_specs = (
        P("vel", "cell"),
        P("vel", None, None),
        P("vel", None, None),
        P("vel", None, None),
        P("vel", None, None, None),
        P(None, None, "vel", None),
        P(None, None, "vel", None),
        P(None, None, "vel"),
    )
    out_specs = (P("vel", "cell"), P("vel", "cell"))
    return jax.shard_map(
        on_device, mesh=mesh, in_specs=in_specs, out_specs=out_specs, check_vma=False
    )
```

```python
import functools

import jax
import jax.numpy as jnp
from jax import lax
from jax.experimental import pallas as pl
from jax.experimental.pallas import tpu as pltpu
from jax.sharding import PartitionSpec as P

VSIDE = 24
MESH = pl.DeviceIdType.MESH
ROWS = 864
HALF = 432
KPAD = 512
F32 = jnp.float32
BF16 = jnp.bfloat16


def split(value):
    high = value.astype(BF16)
    return high, (value - high.astype(F32)).astype(BF16)


def kernel(
    dist_hbm, first, second, weight, picks, target_hbm, coef_hbm, counts,
    out_step, out_gain, out_loss,
    dist, target, coef, columns, edge_out, edge_in, packed, ring, sends_idx, idx, pairs, args, wts, xs, ys, lossq, lossq_row, gain, loss, final, own,
    edge_s, edge_r, part_s, part_r, ring_s, ring_r, zidx_s, zidx_r, xs_s, xs_r, cs_s, cs_r, fin_s, fin_r, local,
):
    vel = lax.axis_index("vel")
    cell = lax.axis_index("cell")
    z = vel // 2
    x = vel % 2
    y = 1 - x
    core = cell % 2
    left = (cell + 15) % 16
    right = (cell + 1) % 16

    def at_z(steps, col=None):
        return {"vel": ((z + steps + 8) % 8) * 2 + (x if col is None else col)}

    partner = at_z(0, y)
    sibling = {"cell": cell + 1 - 2 * core}
    barrier = pltpu.get_barrier_semaphore()
    for steps in range(1, 8):
        pl.semaphore_signal(barrier, inc=1, device_id=at_z(steps), device_id_type=MESH)
    pl.semaphore_signal(barrier, inc=1, device_id=partner, device_id_type=MESH)
    for side in (left, right):
        pl.semaphore_signal(barrier, inc=1, device_id={"cell": side}, device_id_type=MESH)

    def send(src, dst, s_sem, r_sem, device):
        copy = pltpu.make_async_remote_copy(
            src_ref=src, dst_ref=dst, send_sem=s_sem, recv_sem=r_sem, device_id=device, device_id_type=MESH
        )
        copy.start()
        return copy

    loads = [
        pltpu.make_async_copy(src, dst, local.at[i])
        for i, (src, dst) in enumerate(((dist_hbm, dist), (target_hbm, target), (coef_hbm, coef)))
    ]
    for load in loads:
        load.start()

    lane8 = lax.broadcasted_iota(jnp.int32, (8, 128), 1)
    sub8 = lax.broadcasted_iota(jnp.int32, (8, 128), 0)
    lane_first = lane8 < 64
    for b in range(8):
        groups = [2 * b + (half + x) % 2 for half in range(2)]
        take = jnp.concatenate([picks[0, group, pl.ds(core, 8, stride=2), :] for group in groups], axis=1)
        low = take & 127
        upper = take >= 128
        for kind, table in enumerate((first, second, weight)):
            rows = []
            for group in groups:
                row = table[0, pl.ds(group, 1), :]
                for part in range(2):
                    piece = jnp.broadcast_to(row[:, part * 128 : part * 128 + 128], (8, 128))
                    rows.append(jnp.take_along_axis(piece, low, axis=1, mode="promise_in_bounds"))
            value = jnp.where(
                lane_first, jnp.where(upper, rows[1], rows[0]), jnp.where(upper, rows[3], rows[2])
            ).astype(F32)
            for owner in range(8):
                sends_idx[owner, kind * 8 + b : kind * 8 + b + 1, :] = value[owner : owner + 1]

    pl.semaphore_wait(barrier, 10)
    z_copies = [
        send(sends_idx.at[(z + k) % 8], idx.at[core, x, z], zidx_s.at[k], zidx_r.at[k], at_z(k)) for k in range(1, 8)
    ]
    idx[core, x, pl.ds(z, 1)] = sends_idx[pl.ds(z, 1)]

    loads[0].wait()
    pick = jnp.where(lane8 == 127 * sub8, 1.0, 0.0).astype(F32)
    edges = lax.dot_general(
        pick, dist[...], (((1,), (1,)), ((), ())), precision=lax.Precision.HIGHEST, preferred_element_type=F32
    )
    edge_out[0] = edges[1:2]
    edge_out[1] = edges[0:1]
    edge_copies = [
        send(edge_out.at[0], edge_in.at[0], edge_s.at[0], edge_r.at[0], {"cell": right}),
        send(edge_out.at[1], edge_in.at[1], edge_s.at[1], edge_r.at[1], {"cell": left}),
    ]

    for half in range(2):
        rows = slice(half * 8, half * 8 + 8)
        pairs[half, x, 0] = first[0, rows, :].astype(F32)
        pairs[half, x, 1] = second[0, rows, :].astype(F32)
        pairs[half, x, 2] = weight[0, rows, :]
    pairs_copy = send(pairs.at[core, x], pairs.at[core, x], xs_s.at[0], xs_r.at[0], partner)

    node = vel * ROWS + lax.broadcasted_iota(jnp.int32, (ROWS, 128), 0)
    courant = (2 * (node // (VSIDE * VSIDE)) - VSIDE + 1).astype(F32) / (2.0 * VSIDE)
    lane = lax.broadcasted_iota(jnp.int32, (ROWS, 128), 1)
    here = dist[...]
    for copy in z_copies:
        copy.wait_recv()
    idx_copy = send(idx.at[core, x], idx.at[core, x], xs_s.at[2], xs_r.at[2], partner)
    for copy in edge_copies:
        copy.wait_recv()

    def column(row):
        return jnp.broadcast_to(row, (8, ROWS)).T[:, 0:1]

    before = jnp.where(lane == 0, column(edge_in[0]), pltpu.roll(here, 1, axis=1))
    after = jnp.where(lane == 127, column(edge_in[1]), pltpu.roll(here, 127, axis=1))
    change = jnp.maximum(courant, 0.0) * (here - before) + jnp.minimum(courant, 0.0) * (after - here)
    moved = here - change
    out_step[...] = change
    top, low = moved[:HALF], moved[HALF:]
    lane_low = lax.broadcasted_iota(jnp.int32, (HALF, 128), 1) < 64
    packed[0] = jnp.where(lane_low, top, pltpu.roll(low, 64, axis=1))
    packed[1] = jnp.where(lane_low, pltpu.roll(top, 64, axis=1), low)

    def ring_copy(way, step, src_m, dst_m, group):
        return pltpu.make_async_remote_copy(
            src_ref=ring.at[src_m, group],
            dst_ref=ring.at[dst_m, group],
            send_sem=ring_s.at[way, step],
            recv_sem=ring_r.at[way, step],
            device_id=at_z(1 - 2 * way),
            device_id_type=MESH,
        )

    ring[0, pl.ds(x, 1)] = packed[pl.ds(x, 1)]
    ring_copy(0, 1, 0, 1, x).start()
    ring_copy(1, 1, 0, 2, x).start()
    part_copy = send(packed.at[y], ring.at[0, x], part_s, part_r, partner)

    gain[...] = jnp.zeros_like(gain)
    loss[...] = jnp.zeros_like(loss)
    wts[...] = jnp.zeros_like(wts)
    idx_copy.wait_recv()
    idx_on = send(idx.at[core], idx.at[core], cs_s.at[2], cs_r.at[2], sibling)
    pairs_copy.wait_recv()
    pairs_on = send(pairs.at[core, y], pairs.at[core, y], cs_s.at[0], cs_r.at[0], sibling)

    loads[1].wait()
    loads[2].wait()
    columns[:, 0:16] = counts[:, 0, :].T
    live = [columns[pl.ds(tile, 8, stride=2), :] for tile in range(2)]
    slot = lax.broadcasted_iota(jnp.int32, (8, 64), 1)
    for a in range(8):
        for tile in range(2):
            every = pl.ds(tile, 8, stride=2)
            sources = [2 * a + (half + tile) % 2 for half in range(2)]
            start = a * 16 + tile * 8
            args[0, x, start : start + 8] = jnp.concatenate(
                [jnp.where(slot < live[tile][:, s : s + 1], coef[s, every, 0, :], 0.0) for s in sources], axis=1
            )
            args[1, x, start : start + 8] = jnp.concatenate(
                [target[s, every, 0, :] for s in sources], axis=1
            ).astype(F32)
    args_copy = send(args.at[core, x], args.at[core, x], xs_s.at[1], xs_r.at[1], partner)

    part_copy.wait_recv()
    ring_copy(0, 2, 0, 1, y).start()
    ring_copy(1, 2, 0, 2, y).start()
    pairs_on.wait_recv()
    idx_on.wait_recv()

    def args_on():
        return pltpu.make_async_remote_copy(
            src_ref=args.at[core, y], dst_ref=args.at[core, y], send_sem=cs_s.at[1], recv_sem=cs_r.at[1],
            device_id=sibling, device_id_type=MESH,
        )

    def place(m):
        return (z + (m % 2) * (8 - (m + 1) // 2) + (1 - m % 2) * (m // 2)) % 8

    row_low = lax.broadcasted_iota(jnp.int32, (1, 128), 1) < 64

    def split_terms(term, upper):
        high, rest = split(jnp.concatenate([jnp.where(upper, 0.0, term), jnp.where(upper, term, 0.0)], axis=0))
        return jnp.concatenate([high, rest], axis=0)

    def gather_group(i, m, group, sequence, e):
        zz = place(m)
        actual = 2 * zz + group
        rows = [idx[e, group, zz, b : b + 1, :] for b in range(8)]
        for a in range(8):
            even = idx[e, 0, a, pl.ds(8 + zz, 1), :]
            odd = idx[e, 1, a, pl.ds(8 + zz, 1), :]
            rows.append(jnp.where(row_low == (group == 0), even, odd))
        pair_half, pair_row = zz // 4, pl.ds(actual % 8, 1)
        rows.append(pairs[pair_half, e, 1, pair_row, :])
        nodes = jnp.concatenate(rows, axis=1)
        upper = nodes >= float(HALF)
        local = jnp.where(upper, nodes - float(HALF), nodes)
        slot_iota = lax.broadcasted_iota(jnp.int32, (KPAD, 18 * 128), 0).astype(F32)
        one_hot = jnp.where(slot_iota == local, 1.0, 0.0).astype(BF16)
        found = jnp.dot(wts[i], one_hot, preferred_element_type=F32)
        found = found[0:128] + found[128:256]
        found = jnp.where(upper, found[64:128], found[0:64])
        for b in range(8):
            scale = idx[e, group, zz, 16 + b : 17 + b, :]
            xs[m, group, e, b] = found[:, b * 128 : b * 128 + 128] * scale
            ys[m, group, e, b] = found[:, 1024 + b * 128 : 1024 + b * 128 + 128]
        share = pairs[pair_half, e, 2, pair_row, :]
        goal = pairs[pair_half, e, 0, pair_row, :]
        upper = goal >= float(HALF)
        terms = split_terms(found[:, 2048:2304] * share, upper)
        goal = jnp.where(upper, goal - float(HALF), goal)
        for part in range(2):
            tile = (sequence % 4) * 2 + part
            lossq[e, tile] = terms[:, part * 128 : part * 128 + 128]
            lossq_row[e, tile] = goal[:, part * 128 : part * 128 + 128]

    def scatter(goals, terms):
        goal = jnp.concatenate(goals, axis=1)
        node_iota = lax.broadcasted_iota(jnp.int32, (HALF, len(goals) * 128), 0).astype(F32)
        one_hot = jnp.where(node_iota == goal, 1.0, 0.0).astype(BF16)
        return lax.dot_general(
            one_hot, jnp.concatenate(terms, axis=1), (((1,), (1,)), ((), ())), preferred_element_type=F32
        )

    tile_low = lax.broadcasted_iota(jnp.int32, (64, 128), 1) < 64

    def chunk(c, e):
        goals, terms = [], []
        for i in range(8):
            n = c * 8 + i
            m = sum([(n + 64 - k * k) // 64 for k in range(1, 8)])
            d = n - m * m
            later = (d + 7 - m) // 8
            ma = (1 - later) * m + later * (d - m - 1)
            mb = (1 - later) * d + later * m
            za, zb = place(ma), place(mb)
            even, odd = xs[ma, 0, e, zb], xs[ma, 1, e, zb]
            for tile in range(2):
                mine = jnp.where(tile_low, even, odd) if tile == 0 else jnp.where(tile_low, odd, even)
                row = pl.ds(za * 16 + tile * 8 + zb, 1)
                goal = args[1, e, row, :]
                upper = goal >= float(HALF)
                terms.append(split_terms(mine * ys[mb, tile, e, za] * args[0, e, row, :], upper))
                goals.append(jnp.where(upper, goal - float(HALF), goal))
        gain[e] += scatter(goals, terms)
        return e

    def finish(e, where):
        g = gain[e]
        s = loss[e]
        where[0] = g[:, 0:128] + g[:, 128:256]
        where[1] = ring[0, e] * (s[:, 0:128] + s[:, 128:256])

    def final_copy():
        return pltpu.make_async_remote_copy(
            src_ref=packed.at[0], dst_ref=final.at[x], send_sem=fin_s, recv_sem=fin_r, device_id=partner,
            device_id_type=MESH,
        )

    part_copy.wait_send()

    def step(t, carry):
        k = (t + 1) // 2
        group = (x + t + 1) % 2
        last = t // 7

        @pl.when(t >= 1)
        def _():
            m0 = 2 * k - 1
            m1 = 2 * k - last
            ring_copy(0, t, m0, m0, (1 - last) * group).wait_recv()
            ring_copy(1, t, m1, m1, (1 - last) * group + last).wait_recv()

        @pl.when((t >= 1) & (t <= 4))
        def _():
            ring_copy(0, t + 2, 2 * k - 1, 2 * k + 1, group).start()
            ring_copy(1, t + 2, 2 * k, 2 * k + 2, group).start()

        @pl.when((t >= 5) & (t <= 6))
        def _():
            ring_copy(group, 7, 5 + group, 7, group).start()

        @pl.when(t == 1)
        def _():
            args_copy.wait_recv()
            args_on().start()

        @pl.when(t == 2)
        def _():
            args_on().wait_recv()

        ends = last + (7 - t) // 7
        arrived = []
        for i in range(2):
            m = (1 - ends) * (2 * k - 1 + i) + last * 7
            g = (1 - ends) * group + ends * i
            arrived.append((m, g))
            high, rest = split(ring[m, g].T)
            wts[i, 0:128, 0:HALF] = high
            wts[i, 128:256, 0:HALF] = rest

        def ready(t):
            return (t // 2) * (t // 2 + 1) // 2 + 2 * (t // 7)

        from_chunk = ready(t - 1 + (7 - t) // 7)

        def one_owner(turn, inner):
            e = (y + turn) % 2
            for i in range(2):
                gather_group(i, *arrived[i], 2 * t + i, e)

            @pl.when(t % 2 == 1)
            def _():
                loss[e] += scatter([lossq_row[e, i] for i in range(8)], [lossq[e, i] for i in range(8)])

            lax.fori_loop(from_chunk, ready(t), chunk, e)

            @pl.when((t == 7) & (turn == 0))
            def _():
                finish(y, packed)
                packed[0] = packed[0] - packed[1]
                final_copy().start()

            return inner

        lax.fori_loop(0, 2, one_owner, 0)
        return carry

    lax.fori_loop(0, 8, step, 0)

    finish(x, own)
    final_copy().wait_recv()

    def unpacked(mine, theirs, ref):
        lo = jnp.where(x == 0, mine, theirs)
        hi = jnp.where(x == 0, theirs, mine)
        ref[0:HALF, :] = jnp.where(lane_low, lo, pltpu.roll(hi, 64, axis=1))
        ref[HALF:ROWS, :] = jnp.where(lane_low, pltpu.roll(lo, 64, axis=1), hi)

    unpacked(own[0], final[y], out_gain)
    unpacked(own[1], jnp.zeros((HALF, 128), F32), out_loss)

    final_copy().wait_send()
    for copy in edge_copies + z_copies + [pairs_copy, args_copy, idx_copy, pairs_on, args_on(), idx_on]:
        copy.wait_send()

    def drain(t, carry):
        ring_copy(0, t, 0, 0, 0).wait_send()
        ring_copy(1, t, 0, 0, 0).wait_send()
        return carry

    lax.fori_loop(1, 8, drain, 0)


def on_device(distribution, pair_first, pair_second, pair_weight, proj_pair, proj_target, proj_coef, slot_counts):
    vmem = pl.BlockSpec(memory_space=pltpu.VMEM)
    hbm = pl.BlockSpec(memory_space=pl.ANY)
    dma = pltpu.SemaphoreType.DMA
    block = jax.ShapeDtypeStruct((ROWS, 128), F32)
    change, gain, loss = pl.pallas_call(
        kernel,
        out_shape=(block, block, block),
        in_specs=[hbm, vmem, vmem, vmem, vmem, hbm, hbm, vmem],
        out_specs=(vmem, vmem, vmem),
        scratch_shapes=[
            pltpu.VMEM((ROWS, 128), F32),
            pltpu.VMEM((16, 16, 1, 64), jnp.int32),
            pltpu.VMEM((16, 16, 1, 64), F32),
            pltpu.VMEM((16, 128), jnp.int32),
            pltpu.VMEM((2, 1, ROWS), F32),
            pltpu.VMEM((2, 1, ROWS), F32),
            pltpu.VMEM((2, HALF, 128), F32),
            pltpu.VMEM((8, 2, HALF, 128), F32),
            pltpu.VMEM((8, 24, 128), F32),
            pltpu.VMEM((2, 2, 8, 24, 128), F32),
            pltpu.VMEM((2, 2, 3, 8, 256), F32),
            pltpu.VMEM((2, 2, 128, 128), F32),
            pltpu.VMEM((2, 256, KPAD), BF16),
            pltpu.VMEM((8, 2, 2, 8, 64, 128), F32),
            pltpu.VMEM((8, 2, 2, 8, 64, 128), F32),
            pltpu.VMEM((2, 8, 256, 128), BF16),
            pltpu.VMEM((2, 8, 1, 128), F32),
            pltpu.VMEM((2, HALF, 256), F32),
            pltpu.VMEM((2, HALF, 256), F32),
            pltpu.VMEM((2, HALF, 128), F32),
            pltpu.VMEM((2, HALF, 128), F32),
            dma((2,)), dma((2,)), dma, dma, dma((2, 8)), dma((2, 8)), dma((8,)), dma((8,)), dma((3,)), dma((3,)),
            dma((3,)), dma((3,)), dma, dma,
            dma((3,)),
        ],
        compiler_params=pltpu.CompilerParams(
            collective_id=0, has_side_effects=True, vmem_limit_bytes=60 << 20
        ),
    )(
        distribution, pair_first, pair_second, pair_weight, proj_pair, proj_target, proj_coef,
        slot_counts.transpose(0, 2, 1),
    )
    return distribution - change, gain - loss


def solution(mesh):
    in_specs = (
        P("vel", "cell"),
        P("vel", None, None),
        P("vel", None, None),
        P("vel", None, None),
        P("vel", None, None, None),
        P(None, None, "vel", None),
        P(None, None, "vel", None),
        P(None, None, "vel"),
    )
    out_specs = (P("vel", "cell"), P("vel", "cell"))
    return jax.shard_map(
        on_device, mesh=mesh, in_specs=in_specs, out_specs=out_specs, check_vma=False
    )
```

```python
import functools

import jax
import jax.numpy as jnp
from jax import lax
from jax.experimental import pallas as pl
from jax.experimental.pallas import tpu as pltpu
from jax.sharding import PartitionSpec as P

VSIDE = 24
MESH = pl.DeviceIdType.MESH
ROWS = 864
HALF = 432
KPAD = 512
F32 = jnp.float32
BF16 = jnp.bfloat16


def split(value):
    high = value.astype(BF16)
    return high, (value - high.astype(F32)).astype(BF16)


def kernel(
    dist_hbm, first_hbm, second_hbm, weight_hbm, picks_hbm, target_hbm, coef_hbm, counts_hbm,
    out_step, out_gain, out_loss,
    dist, target, coef, first, second, weight, picks, counts,
    columns, edge_out, edge_in, edge_row, ring_edge, packed, ring, sends_idx, idx, pairs, args, wts, xs, ys, lossq, lossq_row, gain, loss, final, own,
    edge_s, edge_r, part_s, part_r, ring_s, ring_r, zidx_s, zidx_r, xs_s, xs_r, cs_s, cs_r, fin_s, fin_r, local, redge_s, redge_r, pedge_s, pedge_r,
):
    vel = lax.axis_index("vel")
    cell = lax.axis_index("cell")
    z = vel // 2
    x = vel % 2
    y = 1 - x
    core = cell % 2
    left = (cell + 15) % 16
    right = (cell + 1) % 16

    def at_z(steps, col=None):
        return {"vel": ((z + steps + 8) % 8) * 2 + (x if col is None else col)}

    partner = at_z(0, y)
    sibling = {"cell": cell + 1 - 2 * core}
    barrier = pltpu.get_barrier_semaphore()
    for steps in range(1, 8):
        pl.semaphore_signal(barrier, inc=1, device_id=at_z(steps), device_id_type=MESH)
    pl.semaphore_signal(barrier, inc=1, device_id=partner, device_id_type=MESH)
    for side in (left, right):
        pl.semaphore_signal(barrier, inc=1, device_id={"cell": side}, device_id_type=MESH)

    def send(src, dst, s_sem, r_sem, device):
        copy = pltpu.make_async_remote_copy(
            src_ref=src, dst_ref=dst, send_sem=s_sem, recv_sem=r_sem, device_id=device, device_id_type=MESH
        )
        copy.start()
        return copy

    loads = [
        pltpu.make_async_copy(src, dst, local.at[i])
        for i, (src, dst) in enumerate(
            (
                (picks_hbm, picks), (first_hbm, first), (second_hbm, second), (weight_hbm, weight), (dist_hbm, dist),
                (counts_hbm, counts), (target_hbm, target), (coef_hbm, coef),
            )
        )
    ]
    for load in loads:
        load.start()
    for load in loads[:4]:
        load.wait()

    lane8 = lax.broadcasted_iota(jnp.int32, (8, 128), 1)
    sub8 = lax.broadcasted_iota(jnp.int32, (8, 128), 0)
    lane_first = lane8 < 64
    for b in range(8):
        groups = [2 * b + (half + x) % 2 for half in range(2)]
        take = jnp.concatenate([picks[0, group, pl.ds(core, 8, stride=2), :] for group in groups], axis=1)
        low = take & 127
        upper = take >= 128
        for kind, table in enumerate((first, second, weight)):
            rows = []
            for group in groups:
                row = table[0, pl.ds(group, 1), :]
                for part in range(2):
                    piece = jnp.broadcast_to(row[:, part * 128 : part * 128 + 128], (8, 128))
                    rows.append(jnp.take_along_axis(piece, low, axis=1, mode="promise_in_bounds"))
            value = jnp.where(
                lane_first, jnp.where(upper, rows[1], rows[0]), jnp.where(upper, rows[3], rows[2])
            ).astype(F32)
            for owner in range(8):
                sends_idx[owner, kind * 8 + b : kind * 8 + b + 1, :] = value[owner : owner + 1]

    loads[4].wait()
    node = vel * ROWS + lax.broadcasted_iota(jnp.int32, (ROWS, 128), 0)
    courant = (2 * (node // (VSIDE * VSIDE)) - VSIDE + 1).astype(F32) / (2.0 * VSIDE)
    positive, negative = jnp.maximum(courant, 0.0), jnp.minimum(courant, 0.0)
    lane = lax.broadcasted_iota(jnp.int32, (ROWS, 128), 1)
    lane_low = lax.broadcasted_iota(jnp.int32, (HALF, 128), 1) < 64
    here = dist[...]
    moved = here - (
        positive * (here - pltpu.roll(here, 1, axis=1)) + negative * (pltpu.roll(here, 127, axis=1) - here)
    )
    top, low = moved[:HALF], moved[HALF:]
    packed[0] = jnp.where(lane_low, top, pltpu.roll(low, 64, axis=1))
    packed[1] = jnp.where(lane_low, pltpu.roll(top, 64, axis=1), low)
    ring[0, pl.ds(x, 1)] = packed[pl.ds(x, 1)]

    pl.semaphore_wait(barrier, 10)
    z_copies = [
        send(sends_idx.at[(z + k) % 8], idx.at[core, x, z], zidx_s.at[k], zidx_r.at[k], at_z(k)) for k in range(1, 8)
    ]

    def ring_copy(way, step, src_m, dst_m, group):
        return pltpu.make_async_remote_copy(
            src_ref=ring.at[src_m, group],
            dst_ref=ring.at[dst_m, group],
            send_sem=ring_s.at[way, step],
            recv_sem=ring_r.at[way, step],
            device_id=at_z(1 - 2 * way),
            device_id_type=MESH,
        )

    def edge_copy(way, step, src_m, dst_m, group):
        return pltpu.make_async_remote_copy(
            src_ref=ring_edge.at[src_m, group],
            dst_ref=ring_edge.at[dst_m, group],
            send_sem=redge_s.at[way, step],
            recv_sem=redge_r.at[way, step],
            device_id=at_z(1 - 2 * way),
            device_id_type=MESH,
        )

    ring_copy(0, 1, 0, 1, x).start()
    ring_copy(1, 1, 0, 2, x).start()
    part_copy = send(packed.at[y], ring.at[0, x], part_s, part_r, partner)
    idx[core, x, pl.ds(z, 1)] = sends_idx[pl.ds(z, 1)]

    pick = jnp.where(lane8 == sub8 + jnp.where(sub8 < 2, 0, 124), 1.0, 0.0).astype(F32)
    pick = jnp.where(sub8 < 4, pick, 0.0)
    halves = [
        lax.dot_general(
            pick, dist[part * HALF : part * HALF + HALF, :], (((1,), (1,)), ((), ())),
            precision=lax.Precision.HIGHEST, preferred_element_type=F32,
        )
        for part in range(2)
    ]
    near = [jnp.concatenate([half[i : i + 1] for half in halves], axis=0) for i in range(4)]
    edge_out[0] = near[3]
    edge_out[1] = near[0]
    edge_copies = [
        send(edge_out.at[0], edge_in.at[0], edge_s.at[0], edge_r.at[0], {"cell": right}),
        send(edge_out.at[1], edge_in.at[1], edge_s.at[1], edge_r.at[1], {"cell": left}),
    ]

    for half in range(2):
        rows = slice(half * 8, half * 8 + 8)
        pairs[half, x, 0] = first[0, rows, :].astype(F32)
        pairs[half, x, 1] = second[0, rows, :].astype(F32)
        pairs[half, x, 2] = weight[0, rows, :]
    pairs_copy = send(pairs.at[core, x], pairs.at[core, x], xs_s.at[0], xs_r.at[0], partner)

    for copy in z_copies:
        copy.wait_recv()
    idx_copy = send(idx.at[core, x], idx.at[core, x], xs_s.at[2], xs_r.at[2], partner)

    for copy in edge_copies:
        copy.wait_recv()
    row_node = (
        vel * ROWS
        + lax.broadcasted_iota(jnp.int32, (2, HALF), 0) * HALF
        + lax.broadcasted_iota(jnp.int32, (2, HALF), 1)
    )
    row_courant = (2 * (row_node // (VSIDE * VSIDE)) - VSIDE + 1).astype(F32) / (2.0 * VSIDE)
    row_positive, row_negative = jnp.maximum(row_courant, 0.0), jnp.minimum(row_courant, 0.0)
    edge_row[0] = near[0] - (row_positive * (near[0] - edge_in[0]) + row_negative * (near[1] - near[0]))
    edge_row[1] = near[3] - (row_positive * (near[3] - near[2]) + row_negative * (edge_in[1] - near[3]))
    ring_edge[0, pl.ds(x, 1)] = edge_row[pl.ds(x, 1)]
    edge_copy(0, 1, 0, 1, x).start()
    edge_copy(1, 1, 0, 2, x).start()
    pedge_copy = send(edge_row.at[y], ring_edge.at[0, x], pedge_s, pedge_r, partner)

    def column(rows):
        return jnp.broadcast_to(rows, (8, HALF)).T[:, 0:1]

    def full_column(rows):
        return jnp.concatenate([column(rows[0:1]), column(rows[1:2])], axis=0)

    before = jnp.where(lane == 0, full_column(edge_in[0]), pltpu.roll(here, 1, axis=1))
    after = jnp.where(lane == 127, full_column(edge_in[1]), pltpu.roll(here, 127, axis=1))
    out_step[...] = positive * (here - before) + negative * (after - here)

    gain[...] = jnp.zeros_like(gain)
    loss[...] = jnp.zeros_like(loss)
    wts[...] = jnp.zeros_like(wts)
    idx_copy.wait_recv()
    idx_on = send(idx.at[core], idx.at[core], cs_s.at[2], cs_r.at[2], sibling)
    pairs_copy.wait_recv()
    pairs_on = send(pairs.at[core, y], pairs.at[core, y], cs_s.at[0], cs_r.at[0], sibling)

    for load in loads[5:]:
        load.wait()
    columns[:, 0:16] = counts[:, 0, :].T
    live = [columns[pl.ds(tile, 8, stride=2), :] for tile in range(2)]
    slot = lax.broadcasted_iota(jnp.int32, (8, 64), 1)
    for a in range(8):
        for tile in range(2):
            every = pl.ds(tile, 8, stride=2)
            sources = [2 * a + (half + tile) % 2 for half in range(2)]
            start = a * 16 + tile * 8
            args[0, x, start : start + 8] = jnp.concatenate(
                [jnp.where(slot < live[tile][:, s : s + 1], coef[s, every, 0, :], 0.0) for s in sources], axis=1
            )
            args[1, x, start : start + 8] = jnp.concatenate(
                [target[s, every, 0, :] for s in sources], axis=1
            ).astype(F32)
    args_copy = send(args.at[core, x], args.at[core, x], xs_s.at[1], xs_r.at[1], partner)

    part_copy.wait_recv()
    ring_copy(0, 2, 0, 1, y).start()
    ring_copy(1, 2, 0, 2, y).start()
    pedge_copy.wait_recv()
    edge_copy(0, 2, 0, 1, y).start()
    edge_copy(1, 2, 0, 2, y).start()
    pairs_on.wait_recv()
    idx_on.wait_recv()

    def args_on():
        return pltpu.make_async_remote_copy(
            src_ref=args.at[core, y], dst_ref=args.at[core, y], send_sem=cs_s.at[1], recv_sem=cs_r.at[1],
            device_id=sibling, device_id_type=MESH,
        )

    def place(m):
        return (z + (m % 2) * (8 - (m + 1) // 2) + (1 - m % 2) * (m // 2)) % 8

    row_low = lax.broadcasted_iota(jnp.int32, (1, 128), 1) < 64

    def split_terms(term, upper):
        high, rest = split(jnp.concatenate([jnp.where(upper, 0.0, term), jnp.where(upper, term, 0.0)], axis=0))
        return jnp.concatenate([high, rest], axis=0)

    def gather_group(i, m, group, sequence, e):
        zz = place(m)
        actual = 2 * zz + group
        rows = [idx[e, group, zz, b : b + 1, :] for b in range(8)]
        for a in range(8):
            even = idx[e, 0, a, pl.ds(8 + zz, 1), :]
            odd = idx[e, 1, a, pl.ds(8 + zz, 1), :]
            rows.append(jnp.where(row_low == (group == 0), even, odd))
        pair_half, pair_row = zz // 4, pl.ds(actual % 8, 1)
        rows.append(pairs[pair_half, e, 1, pair_row, :])
        nodes = jnp.concatenate(rows, axis=1)
        upper = nodes >= float(HALF)
        local = jnp.where(upper, nodes - float(HALF), nodes)
        slot_iota = lax.broadcasted_iota(jnp.int32, (KPAD, 18 * 128), 0).astype(F32)
        one_hot = jnp.where(slot_iota == local, 1.0, 0.0).astype(BF16)
        found = jnp.dot(wts[i], one_hot, preferred_element_type=F32)
        found = found[0:128] + found[128:256]
        found = jnp.where(upper, found[64:128], found[0:64])
        for b in range(8):
            scale = idx[e, group, zz, 16 + b : 17 + b, :]
            xs[m, group, e, b] = found[:, b * 128 : b * 128 + 128] * scale
            ys[m, group, e, b] = found[:, 1024 + b * 128 : 1024 + b * 128 + 128]
        share = pairs[pair_half, e, 2, pair_row, :]
        goal = pairs[pair_half, e, 0, pair_row, :]
        upper = goal >= float(HALF)
        terms = split_terms(found[:, 2048:2304] * share, upper)
        goal = jnp.where(upper, goal - float(HALF), goal)
        for part in range(2):
            tile = (sequence % 4) * 2 + part
            lossq[e, tile] = terms[:, part * 128 : part * 128 + 128]
            lossq_row[e, tile] = goal[:, part * 128 : part * 128 + 128]

    def scatter(goals, terms):
        goal = jnp.concatenate(goals, axis=1)
        node_iota = lax.broadcasted_iota(jnp.int32, (HALF, len(goals) * 128), 0).astype(F32)
        one_hot = jnp.where(node_iota == goal, 1.0, 0.0).astype(BF16)
        return lax.dot_general(
            one_hot, jnp.concatenate(terms, axis=1), (((1,), (1,)), ((), ())), preferred_element_type=F32
        )

    tile_low = lax.broadcasted_iota(jnp.int32, (64, 128), 1) < 64

    def chunk(c, e):
        goals, terms = [], []
        for i in range(8):
            n = c * 8 + i
            m = sum([(n + 64 - k * k) // 64 for k in range(1, 8)])
            d = n - m * m
            later = (d + 7 - m) // 8
            ma = (1 - later) * m + later * (d - m - 1)
            mb = (1 - later) * d + later * m
            za, zb = place(ma), place(mb)
            even, odd = xs[ma, 0, e, zb], xs[ma, 1, e, zb]
            for tile in range(2):
                mine = jnp.where(tile_low, even, odd) if tile == 0 else jnp.where(tile_low, odd, even)
                row = pl.ds(za * 16 + tile * 8 + zb, 1)
                goal = args[1, e, row, :]
                upper = goal >= float(HALF)
                terms.append(split_terms(mine * ys[mb, tile, e, za] * args[0, e, row, :], upper))
                goals.append(jnp.where(upper, goal - float(HALF), goal))
        gain[e] += scatter(goals, terms)
        return e

    def finish(e, where):
        g = gain[e]
        s = loss[e]
        where[0] = g[:, 0:128] + g[:, 128:256]
        lanes = lax.broadcasted_iota(jnp.int32, (HALF, 128), 1)
        value = jnp.where(lanes == 63 * x, column(ring_edge[0, e, 0:1, :]), ring[0, e])
        value = jnp.where(lanes == 63 * x + 64, column(ring_edge[0, e, 1:2, :]), value)
        where[1] = value * (s[:, 0:128] + s[:, 128:256])

    def final_copy():
        return pltpu.make_async_remote_copy(
            src_ref=packed.at[0], dst_ref=final.at[x], send_sem=fin_s, recv_sem=fin_r, device_id=partner,
            device_id_type=MESH,
        )

    cell_row = lax.broadcasted_iota(jnp.int32, (128, HALF), 0)
    part_copy.wait_send()

    def step(t, carry):
        k = (t + 1) // 2
        group = (x + t + 1) % 2
        last = t // 7

        @pl.when(t >= 1)
        def _():
            m0 = 2 * k - 1
            m1 = 2 * k - last
            ring_copy(0, t, m0, m0, (1 - last) * group).wait_recv()
            ring_copy(1, t, m1, m1, (1 - last) * group + last).wait_recv()
            edge_copy(0, t, m0, m0, (1 - last) * group).wait_recv()
            edge_copy(1, t, m1, m1, (1 - last) * group + last).wait_recv()

        @pl.when((t >= 1) & (t <= 4))
        def _():
            ring_copy(0, t + 2, 2 * k - 1, 2 * k + 1, group).start()
            ring_copy(1, t + 2, 2 * k, 2 * k + 2, group).start()
            edge_copy(0, t + 2, 2 * k - 1, 2 * k + 1, group).start()
            edge_copy(1, t + 2, 2 * k, 2 * k + 2, group).start()

        @pl.when((t >= 5) & (t <= 6))
        def _():
            ring_copy(group, 7, 5 + group, 7, group).start()
            edge_copy(group, 7, 5 + group, 7, group).start()

        @pl.when(t == 1)
        def _():
            args_copy.wait_recv()
            args_on().start()

        @pl.when(t == 2)
        def _():
            args_on().wait_recv()

        ends = last + (7 - t) // 7
        arrived = []
        for i in range(2):
            m = (1 - ends) * (2 * k - 1 + i) + last * 7
            g = (1 - ends) * group + ends * i
            arrived.append((m, g))
            turned = ring[m, g].T
            turned = jnp.where(cell_row == 63 * x, ring_edge[m, g, 0:1, :], turned)
            turned = jnp.where(cell_row == 63 * x + 64, ring_edge[m, g, 1:2, :], turned)
            high, rest = split(turned)
            wts[i, 0:128, 0:HALF] = high
            wts[i, 128:256, 0:HALF] = rest

        def ready(t):
            return (t // 2) * (t // 2 + 1) // 2 + 2 * (t // 7)

        from_chunk = ready(t - 1 + (7 - t) // 7)

        def one_owner(turn, inner):
            e = (y + turn) % 2
            for i in range(2):
                gather_group(i, *arrived[i], 2 * t + i, e)

            @pl.when(t % 2 == 1)
            def _():
                loss[e] += scatter([lossq_row[e, i] for i in range(8)], [lossq[e, i] for i in range(8)])

            lax.fori_loop(from_chunk, ready(t), chunk, e)

            @pl.when((t == 7) & (turn == 0))
            def _():
                finish(y, packed)
                packed[0] = packed[0] - packed[1]
                final_copy().start()

            return inner

        lax.fori_loop(0, 2, one_owner, 0)
        return carry

    lax.fori_loop(0, 8, step, 0)

    finish(x, own)
    final_copy().wait_recv()

    def unpacked(mine, theirs, ref):
        lo = jnp.where(x == 0, mine, theirs)
        hi = jnp.where(x == 0, theirs, mine)
        ref[0:HALF, :] = jnp.where(lane_low, lo, pltpu.roll(hi, 64, axis=1))
        ref[HALF:ROWS, :] = jnp.where(lane_low, pltpu.roll(lo, 64, axis=1), hi)

    unpacked(own[0], final[y], out_gain)
    unpacked(own[1], jnp.zeros((HALF, 128), F32), out_loss)

    final_copy().wait_send()
    for copy in edge_copies + z_copies + [pairs_copy, args_copy, idx_copy, pairs_on, args_on(), idx_on, pedge_copy]:
        copy.wait_send()

    def drain(t, carry):
        ring_copy(0, t, 0, 0, 0).wait_send()
        ring_copy(1, t, 0, 0, 0).wait_send()
        edge_copy(0, t, 0, 0, 0).wait_send()
        edge_copy(1, t, 0, 0, 0).wait_send()
        return carry

    lax.fori_loop(1, 8, drain, 0)


def on_device(distribution, pair_first, pair_second, pair_weight, proj_pair, proj_target, proj_coef, slot_counts):
    vmem = pl.BlockSpec(memory_space=pltpu.VMEM)
    hbm = pl.BlockSpec(memory_space=pltpu.HBM)
    dma = pltpu.SemaphoreType.DMA
    block = jax.ShapeDtypeStruct((ROWS, 128), F32)
    change, gain, loss = pl.pallas_call(
        kernel,
        out_shape=(block, block, block),
        in_specs=[hbm] * 8,
        out_specs=(vmem, vmem, vmem),
        scratch_shapes=[
            pltpu.VMEM((ROWS, 128), F32),
            pltpu.VMEM((16, 16, 1, 64), jnp.int32),
            pltpu.VMEM((16, 16, 1, 64), F32),
            pltpu.VMEM((1, 16, 256), jnp.int32),
            pltpu.VMEM((1, 16, 256), jnp.int32),
            pltpu.VMEM((1, 16, 256), F32),
            pltpu.VMEM((1, 16, 16, 64), jnp.int32),
            pltpu.VMEM((16, 1, 16), jnp.int32),
            pltpu.VMEM((16, 128), jnp.int32),
            pltpu.VMEM((2, 2, HALF), F32),
            pltpu.VMEM((2, 2, HALF), F32),
            pltpu.VMEM((2, 2, HALF), F32),
            pltpu.VMEM((8, 2, 2, HALF), F32),
            pltpu.VMEM((2, HALF, 128), F32),
            pltpu.VMEM((8, 2, HALF, 128), F32),
            pltpu.VMEM((8, 24, 128), F32),
            pltpu.VMEM((2, 2, 8, 24, 128), F32),
            pltpu.VMEM((2, 2, 3, 8, 256), F32),
            pltpu.VMEM((2, 2, 128, 128), F32),
            pltpu.VMEM((2, 256, KPAD), BF16),
            pltpu.VMEM((8, 2, 2, 8, 64, 128), F32),
            pltpu.VMEM((8, 2, 2, 8, 64, 128), F32),
            pltpu.VMEM((2, 8, 256, 128), BF16),
            pltpu.VMEM((2, 8, 1, 128), F32),
            pltpu.VMEM((2, HALF, 256), F32),
            pltpu.VMEM((2, HALF, 256), F32),
            pltpu.VMEM((2, HALF, 128), F32),
            pltpu.VMEM((2, HALF, 128), F32),
            dma((2,)), dma((2,)), dma, dma, dma((2, 8)), dma((2, 8)), dma((8,)), dma((8,)), dma((3,)), dma((3,)),
            dma((3,)), dma((3,)), dma, dma,
            dma((8,)), dma((2, 8)), dma((2, 8)), dma, dma,
        ],
        compiler_params=pltpu.CompilerParams(
            collective_id=0, has_side_effects=True, vmem_limit_bytes=60 << 20
        ),
    )(
        distribution, pair_first, pair_second, pair_weight, proj_pair, proj_target, proj_coef,
        slot_counts.transpose(0, 2, 1),
    )
    return distribution - change, gain - loss


def solution(mesh):
    in_specs = (
        P("vel", "cell"),
        P("vel", None, None),
        P("vel", None, None),
        P("vel", None, None),
        P("vel", None, None, None),
        P(None, None, "vel", None),
        P(None, None, "vel", None),
        P(None, None, "vel"),
    )
    out_specs = (P("vel", "cell"), P("vel", "cell"))
    return jax.shard_map(
        on_device, mesh=mesh, in_specs=in_specs, out_specs=out_specs, check_vma=False
    )
```
